32 devices in a mesh: grp: 2 (over x), pos: 16 (over z, y, core).
Axes of the slice: x: 2, y: 2, z: 4, core: 2. Of those that a mesh axis runs over, the one named last changes fastest.
Arguments:
- inputs: bfloat16 [768, 16, 512], P('grp', 'pos'), parts along dimension 0, may hold values from -6 to 6
- cotangent: bfloat16 [768, 16, 512], P('grp', 'pos'), parts along dimension 0, may hold values from -6 to 6
- col_weights: bfloat16 [4, 512, 512], replicated, may hold values from -0.25 to 0.25
- row_weights: bfloat16 [4, 512, 512], replicated, may hold values from -0.25 to 0.25
- read_start: int32 [768], P('grp'), parts along dimension 0, may hold values from 0 to 14, as said below
- read_end: int32 [768], P('grp'), parts along dimension 0, may hold values from 2 to 16, as said below
- windows: int32 [8], replicated, may hold values from 2 to 7
Outputs:
- input_grad: bfloat16 [768, 16, 512], P('grp', 'pos'), parts along dimension 0
- col_weight_grads: float32 [8, 512, 512], P('grp', 'pos'), parts along dimension 0
- row_weight_grads: float32 [8, 512, 512], P('grp', 'pos'), parts along dimension 0
The draws below stay inside these ranges and needn't reach their ends.
There are 2 independent parts, one for each index of `grp`. The reference program is written for one: setup_inputs(seed, part) draws one part's arguments, and reference() takes and returns one part's arrays. A program takes and returns all parts, laid end to end along the dimension named above; an argument that names none is the same for every part. Nothing has to cross between parts.
Inputs may be any that keep to these rules, and one draw needn't show every extreme that they name: Read r covers positions read_start[r] to read_end[r] - 1, a span of 2 positions or more. read_end[r] - read_start[r] >= 2.
All inputs are finite; a program needn't handle non-finite values.
Results may differ from the reference program's by a relative error of at most 0.033.
The reference program's roundings to bfloat16 on the way count: a program that leaves them out, or rounds other values in their place, can miss the bound.
Values may be sent and summed in bfloat16 or wider, within the bound.
A program may use at most 128 MiB of HBM per device.

```python
import jax
import jax.numpy as jnp
from jax import lax

D = 512
HEADS = 8
READS = 384
POSITIONS = 16


def read_spans(key):
    span_key = jax.random.fold_in(key, 11)
    len_key, start_key = jax.random.split(span_key)
    shortest = POSITIONS // 8
    span_len = jax.random.randint(len_key, (READS,), shortest, POSITIONS + 1)
    first_pos = jax.random.randint(start_key, (READS,), 0, POSITIONS - span_len + 1)
    read_ids = jnp.arange(READS)
    span_len = jnp.where(read_ids == 0, POSITIONS, jnp.where(read_ids <= 2, shortest, span_len))
    first_pos = jnp.where(read_ids == 0, 0, jnp.where(read_ids == 1, POSITIONS - shortest, jnp.where(read_ids == 2, 0, first_pos)))
    return (first_pos.astype(jnp.int32), (first_pos + span_len).astype(jnp.int32))


def draw_read_start(key, part):
    return read_spans(key)[0]


def draw_read_end(key, part):
    return read_spans(key)[1]


def touch_ends(values, own_key, low, top_value):
    longest = values.shape.index(max(values.shape))
    spots = []
    for shift in (0, 1):
        where = [jax.random.randint(jax.random.fold_in(own_key, axis), (), 0, length) for axis, length in enumerate(values.shape)]
        where[longest] = (where[longest] + shift) % values.shape[longest]
        spots.append(tuple(where))
    return values.at[spots[0]].set(low).at[spots[1]].set(top_value)


def spiked(values, own_key, source, target, blocks, factor):
    def block_of(position):
        return (jnp.arange(values.shape[position]) // (values.shape[position] // blocks)).reshape((-1,) + (1,) * (values.ndim - 1 - position))

    one_side = jax.random.permutation(own_key, blocks)[block_of(target)]
    far = (block_of(target) + blocks // 2) % blocks
    return jnp.where((block_of(source) == one_side) | (block_of(source) == far), factor * values, values)


def block_scale(key, shape, cuts, smallest, largest):
    loudness = 1.0
    for position, parts in cuts:
        steps = jax.random.uniform(jax.random.fold_in(jax.random.fold_in(key, 6), position), (parts,), jnp.float32, smallest / len(cuts), largest / len(cuts))
        loudness = loudness * jnp.repeat(jnp.exp(steps), shape[position] // parts).reshape((-1,) + (1,) * (len(shape) - 1 - position))
    return loudness


def normal_values(key, shape, spread, most, cuts=(), kind=jnp.bfloat16):
    values = jax.random.normal(key, shape, jnp.float32) * spread
    if len(cuts) > 0:
        values = block_scale(key, shape, cuts, -0.22, 0.18) * values
    return jnp.clip(values, min=-most, max=most).astype(kind)


def heavy_noise(stream_key, shape, scale, most, cuts, heavy, kind=jnp.bfloat16):
    values = scale * jax.random.normal(stream_key, shape, jnp.float32)
    if cuts:
        values = values * block_scale(stream_key, shape, cuts, -0.22, 0.18)
    return jnp.clip(spiked(values, jax.random.fold_in(stream_key, 3), *heavy), -most, most).astype(kind)


def setup_inputs(seed: int = 0, part: int = 0) -> dict:
    key_of = jax.random.split(jax.random.key(seed), 8)
    part_keys = jax.random.split(jax.random.fold_in(key_of[7], part), 8)
    return {
        "inputs": heavy_noise(part_keys[0], (READS, POSITIONS, D), 1.0, 6.0, ((1, 16),), (1, 2, 16, 2.0)),
        "cotangent": normal_values(part_keys[1], (READS, POSITIONS, D), 1.0, 6.0, ((1, 16),)),
        "col_weights": normal_values(key_of[2], (4, D, D), D ** -0.5, 0.25),
        "row_weights": normal_values(key_of[3], (4, D, D), D ** -0.5, 0.25),
        "read_start": draw_read_start(jax.random.fold_in(jax.random.fold_in(key_of[7], part), 71), part),
        "read_end": draw_read_end(jax.random.fold_in(jax.random.fold_in(key_of[7], part), 71), part),
        "windows": touch_ends(jax.random.randint(key_of[6], (HEADS,), 2, POSITIONS // 2), jax.random.fold_in(key_of[6], 1), 2, (POSITIONS // 2) - 1).astype(jnp.int32),
    }


neg_fill = -1e+30

def attend(scores, allowed, value_heads, form):
    masked = jnp.where(allowed, scores, neg_fill)
    highest = lax.stop_gradient(lax.optimization_barrier(jnp.max(masked, axis=-1, keepdims=True)))
    raised = jnp.exp(masked - highest)
    soft_weights = (raised / lax.optimization_barrier(jnp.sum(raised, axis=-1, keepdims=True))).astype(jnp.bfloat16)
    return jnp.einsum(form, soft_weights.astype(jnp.float32), value_heads)

def col_core(queries, key_rows, value_rows, coverage):
    reads, local_pos, width = queries.shape
    heads_shape = (reads, local_pos, HEADS, width // HEADS)
    query_heads = queries.reshape(heads_shape).astype(jnp.float32)
    key_heads = key_rows.reshape(heads_shape).astype(jnp.float32)
    value_heads = value_rows.reshape(heads_shape).astype(jnp.float32)
    scores = jnp.einsum('iphe,jphe->phij', query_heads, key_heads) * (width // HEADS) ** (-0.5)
    allowed = (coverage.T[:, None, None, :] > 0.5) | jnp.eye(reads, dtype=bool)[None, None]
    mixed = attend(scores, allowed, value_heads, 'phij,jphe->iphe')
    return mixed.reshape(queries.shape).astype(jnp.bfloat16)

def row_core(queries, key_rows, value_rows, coverage, windows):
    reads, length, width = queries.shape
    heads_shape = (reads, length, HEADS, width // HEADS)
    query_heads = queries.reshape(heads_shape).astype(jnp.float32)
    key_heads = key_rows.reshape(heads_shape).astype(jnp.float32)
    value_heads = value_rows.reshape(heads_shape).astype(jnp.float32)
    scores = jnp.einsum('bihe,bjhe->bhij', query_heads, key_heads) * (width // HEADS) ** (-0.5)
    places = jnp.arange(length).astype(jnp.int32)
    distance = jnp.abs(places[:, None] - places[None, :])
    in_window = distance[None] <= windows.astype(jnp.int32)[:, None, None]
    covered = (coverage[:, None, None, :] > 0.5) | jnp.eye(length, dtype=bool)[None, None]
    allowed = in_window[None] & covered
    mixed = attend(scores, allowed, value_heads, 'bhij,bjhe->bihe')
    return mixed.reshape(queries.shape).astype(jnp.bfloat16)

def projections(inputs, weights):
    width = inputs.shape[-1]
    flat_rows = inputs.reshape(-1, width)
    return tuple((jnp.dot(flat_rows, weights[which], preferred_element_type=jnp.float32).astype(jnp.bfloat16).reshape(inputs.shape) for which in range(3)))

def branch_forward(inputs, weights, coverage, core_apply):
    width = inputs.shape[-1]
    queries, key_rows, value_rows = projections(inputs, weights)
    mixed = core_apply(queries, key_rows, value_rows)
    output_proj = jnp.dot(mixed.reshape(-1, width), weights[3], preferred_element_type=jnp.float32).reshape(inputs.shape)
    return (inputs.astype(jnp.float32) + output_proj * coverage[..., None]).astype(jnp.bfloat16)

def outer_sum(left, right):
    width = left.shape[-1]
    return jnp.dot(left.reshape(-1, width).T, right.reshape(-1, width), preferred_element_type=jnp.float32)

def branch_backward(inputs, upstream, weights, coverage, core_pullback):
    width = inputs.shape[-1]
    queries, key_rows, value_rows = projections(inputs, weights)
    out_grad = (upstream.astype(jnp.float32) * coverage[..., None]).astype(jnp.bfloat16)
    mixed_grad = jnp.dot(out_grad.reshape(-1, width), weights[3].T, preferred_element_type=jnp.float32).astype(jnp.bfloat16).reshape(inputs.shape)
    mixed, query_grad, key_grad, value_grad = core_pullback(queries, key_rows, value_rows, mixed_grad)
    weight_terms = jnp.stack([outer_sum(inputs, query_grad), outer_sum(inputs, key_grad), outer_sum(inputs, value_grad), outer_sum(mixed, out_grad)])
    back = upstream.astype(jnp.float32).reshape(-1, width)
    for which, grad_part in enumerate((query_grad, key_grad, value_grad)):
        back = back + jnp.dot(grad_part.reshape(-1, width), weights[which].T, preferred_element_type=jnp.float32)
    return (back.reshape(inputs.shape).astype(jnp.bfloat16), weight_terms)

def reference(inputs, cotangent, col_weights, row_weights, read_start, read_end, windows):
    places = jnp.arange(POSITIONS).astype(jnp.int32)
    coverage = ((places[None, :] >= read_start[:, None]) & (places[None, :] < read_end[:, None])).astype(jnp.float32)

    def col_apply(queries, key_rows, value_rows):

        def one_position(items):
            part_q, part_k, part_v, part_c = items
            return col_core(part_q[:, None], part_k[:, None], part_v[:, None], part_c[:, None])[:, 0]
        stacked = lax.map(one_position, (jnp.swapaxes(queries, 0, 1), jnp.swapaxes(key_rows, 0, 1), jnp.swapaxes(value_rows, 0, 1), coverage.T))
        return jnp.swapaxes(stacked, 0, 1)

    def col_pullback(queries, key_rows, value_rows, mixed_grad):

        def one_position(items):
            part_q, part_k, part_v, part_c, part_g = items
            mixed, pull = jax.vjp(lambda first_q, first_k, first_v: col_core(first_q, first_k, first_v, part_c[:, None]), part_q[:, None], part_k[:, None], part_v[:, None])
            grads = pull(part_g[:, None])
            return (mixed[:, 0], grads[0][:, 0], grads[1][:, 0], grads[2][:, 0])
        results = lax.map(one_position, (jnp.swapaxes(queries, 0, 1), jnp.swapaxes(key_rows, 0, 1), jnp.swapaxes(value_rows, 0, 1), coverage.T, jnp.swapaxes(mixed_grad, 0, 1)))
        return tuple((jnp.swapaxes(result, 0, 1) for result in results))

    def row_pullback(queries, key_rows, value_rows, mixed_grad):

        def one_read(items):
            part_q, part_k, part_v, part_c, part_g = items
            mixed, pull = jax.vjp(lambda first_q, first_k, first_v: row_core(first_q, first_k, first_v, part_c[None], windows), part_q[None], part_k[None], part_v[None])
            grads = pull(part_g[None])
            return (mixed[0], grads[0][0], grads[1][0], grads[2][0])
        return lax.map(one_read, (queries, key_rows, value_rows, coverage, mixed_grad))
    hidden = branch_forward(inputs, col_weights, coverage, col_apply)
    hidden_grad, row_weight_grads = branch_backward(hidden, cotangent, row_weights, coverage, row_pullback)
    input_grad, col_weight_grads = branch_backward(inputs, hidden_grad, col_weights, coverage, col_pullback)
    return (input_grad, col_weight_grads, row_weight_grads)
```

```python
import functools

import jax
import jax.numpy as jnp
from jax import lax
from jax.experimental import pallas as pl
from jax.experimental.pallas import tpu as pltpu
from jax.sharding import PartitionSpec as P

HEADS = 8
LANES = 128
NEG = -1e30
FAR = 1e9
VMEM_LIMIT = 56 * 1024 * 1024
f32, bf16 = jnp.float32, jnp.bfloat16


def dot_nn(a, b):
    return lax.dot_general(a, b, (((1,), (0,)), ((), ())), preferred_element_type=f32)


def dot_nt(a, b):
    return lax.dot_general(a, b, (((1,), (1,)), ((), ())), preferred_element_type=f32)


def dot_tn(a, b):
    return lax.dot_general(a, b, (((0,), (0,)), ((), ())), preferred_element_type=f32)


def project(x_ref, w_ref, q_ref, k_ref, v_ref):
    x = x_ref[...]
    q_ref[...] = (dot_nn(x, w_ref[0]) * 0.125).astype(bf16)
    k_ref[...] = dot_nn(x, w_ref[1]).astype(bf16)
    v_ref[...] = dot_nn(x, w_ref[2]).astype(bf16)


def probs_t(k2, qm, dist, width):
    s = jnp.where(dist <= width, dot_nt(k2, qm), NEG)
    e = jnp.exp(s - jnp.max(s, axis=0, keepdims=True))
    return e * (1.0 / jnp.sum(e, axis=0, keepdims=True))


def halves(pair):
    lane = lax.broadcasted_iota(jnp.int32, pair.shape, 1)
    low = lane < LANES // 2
    zero = jnp.zeros_like(pair)
    return jnp.where(low, pair, zero), jnp.where(low, zero, pair)


def merge(a, b):
    lane = lax.broadcasted_iota(jnp.int32, a.shape, 1)
    return jnp.where(lane < LANES // 2, a, b)


def forward_pairs(q_ref, k_ref, v_ref, dist_ref, m_ref):
    @pl.loop(0, HEADS // 2)
    def _(pair):
        at = pl.ds(pl.multiple_of(pair * LANES, LANES), LANES)
        k2, v2 = k_ref[:, at], v_ref[:, at]
        outs = []
        for qm in halves(q_ref[:, at]):
            p = probs_t(k2, qm, dist_ref[...], 0.5).astype(bf16)
            outs.append(dot_tn(p, v2))
        m_ref[:, at] = merge(*outs).astype(bf16)


def backward_pairs(q_ref, k_ref, v_ref, g_ref, dist_ref, width_of, m_ref, dq_ref, dk_ref, dv_ref):
    @pl.loop(0, HEADS // 2)
    def _(pair):
        at = pl.ds(pl.multiple_of(pair * LANES, LANES), LANES)
        k2, v2 = k_ref[:, at], v_ref[:, at]
        q_parts, g_parts = halves(q_ref[:, at]), halves(g_ref[:, at])
        outs, dqs, dk, dv = [], [], 0.0, 0.0
        for which in range(2):
            qm, gm = q_parts[which], g_parts[which]
            p = probs_t(k2, qm, dist_ref[...], width_of(pair * 2 + which))
            pb = p.astype(bf16)
            if m_ref is not None:
                outs.append(dot_tn(pb, v2))
            dp = dot_nt(v2, gm).astype(bf16).astype(f32)
            ds = (p * (dp - jnp.sum(dp * p, axis=0, keepdims=True))).astype(bf16)
            dv = dv + dot_nn(pb, gm)
            dk = dk + dot_nn(ds, qm)
            dqs.append(dot_tn(ds, k2))
        if m_ref is not None:
            m_ref[:, at] = merge(*outs).astype(bf16)
        dq_ref[:, at] = (merge(*dqs) * 0.125).astype(bf16)
        dk_ref[:, at] = dk.astype(bf16)
        dv_ref[:, at] = dv.astype(bf16)


def col_dist(dist_ref, cov):
    n = dist_ref.shape[0]
    j = lax.broadcasted_iota(jnp.int32, (n, n), 0)
    i = lax.broadcasted_iota(jnp.int32, (n, n), 1)
    dist_ref[...] = jnp.where((cov > 0.5) | (i == j), 0.0, FAR)


def finish(x_ref, up_ref, cov, w_ref, m_ref, og_ref, dq_ref, dk_ref, dv_ref, back_ref, terms_ref):
    x = x_ref[...]
    for which, grad_ref in enumerate((dq_ref, dk_ref, dv_ref)):
        terms_ref[which] = dot_tn(x, grad_ref[...]).astype(bf16)
    terms_ref[3] = dot_tn(m_ref[...], og_ref[...]).astype(bf16)


def back_sum(up_ref, w_ref, dq_ref, dk_ref, dv_ref, back_ref):
    back = up_ref[...].astype(f32)
    for which, grad_ref in enumerate((dq_ref, dk_ref, dv_ref)):
        back = back + dot_nt(grad_ref[...], w_ref[which])
    back_ref[...] = back.astype(bf16)


def col_forward(x_ref, w_ref, cov_ref, q_ref, k_ref, v_ref, m_ref, h_ref, dist_ref):
    cov = cov_ref[...]
    col_dist(dist_ref, cov)
    project(x_ref, w_ref, q_ref, k_ref, v_ref)
    forward_pairs(q_ref, k_ref, v_ref, dist_ref, m_ref)
    out = dot_nn(m_ref[...], w_ref[3])
    h_ref[...] = (x_ref[...].astype(f32) + out * cov).astype(bf16)


def row_both(
    h_ref, up_ref, w_ref, cov_ref, sub_ref, lane_ref, windows_ref, back_ref, terms_ref,
    q_ref, k_ref, v_ref, m_ref, og_ref, g_ref, dq_ref, dk_ref, dv_ref, dist_ref,
):
    cov = cov_ref[...]
    gap = jnp.abs(sub_ref[:, 0:1] - lane_ref[0:1, :])
    same = sub_ref[:, 1:2] == lane_ref[1:2, :]
    dist_ref[...] = jnp.where(same & ((cov > 0.5) | (gap == 0.0)), gap, FAR)
    project(h_ref, w_ref, q_ref, k_ref, v_ref)
    og_ref[...] = (up_ref[...].astype(f32) * cov).astype(bf16)
    g_ref[...] = dot_nt(og_ref[...], w_ref[3]).astype(bf16)
    backward_pairs(
        q_ref, k_ref, v_ref, g_ref, dist_ref,
        lambda head: windows_ref[head].astype(f32), m_ref, dq_ref, dk_ref, dv_ref,
    )
    back_sum(up_ref, w_ref, dq_ref, dk_ref, dv_ref, back_ref)
    finish(h_ref, up_ref, cov, w_ref, m_ref, og_ref, dq_ref, dk_ref, dv_ref, back_ref, terms_ref)


def col_backward(
    x_ref, up_ref, w_ref, cov_ref, q_ref, k_ref, v_ref, m_ref, back_ref, terms_ref,
    og_ref, g_ref, dq_ref, dk_ref, dv_ref, dist_ref,
):
    cov = cov_ref[...]
    col_dist(dist_ref, cov)
    og_ref[...] = (up_ref[...].astype(f32) * cov).astype(bf16)
    g_ref[...] = dot_nt(og_ref[...], w_ref[3]).astype(bf16)
    backward_pairs(
        q_ref, k_ref, v_ref, g_ref, dist_ref, lambda head: 0.5, None, dq_ref, dk_ref, dv_ref
    )
    back_sum(up_ref, w_ref, dq_ref, dk_ref, dv_ref, back_ref)
    finish(x_ref, up_ref, cov, w_ref, m_ref, og_ref, dq_ref, dk_ref, dv_ref, back_ref, terms_ref)


def reduce_rows(terms, ranks, me):
    width = terms.shape[-1]
    held = terms.reshape(4, ranks, width // ranks, width)
    bit = 0
    while (1 << bit) < ranks:
        mine = (me >> bit) & 1
        blocks = held.shape[1] // 2
        split = held.reshape(4, blocks, 2, width // ranks, width)
        keep = lax.dynamic_index_in_dim(split, mine, 2, keepdims=False)
        give = lax.dynamic_index_in_dim(split, 1 - mine, 2, keepdims=False)
        got = lax.ppermute(give, "pos", [(r, r ^ (1 << bit)) for r in range(ranks)])
        total = keep.astype(f32) + got.astype(f32)
        bit += 1
        held = total if (1 << bit) >= ranks else total.astype(bf16)
    return held[:, 0]


def shards(inputs, cotangent, col_weights, row_weights, read_start, read_end, windows):
    reads, local_pos, width = inputs.shape
    ranks = lax.axis_size("pos")
    me = lax.axis_index("pos")
    block = reads // ranks
    rows = reads
    x = inputs.reshape(rows, width)
    cov = ((me >= read_start) & (me < read_end)).astype(f32)[:, None]
    start_here = lax.dynamic_slice_in_dim(read_start, me * block, block)
    end_here = lax.dynamic_slice_in_dim(read_end, me * block, block)
    place = jnp.arange(ranks, dtype=jnp.int32)[:, None]
    row_cov = ((place >= start_here[None]) & (place < end_here[None])).astype(f32).reshape(rows, 1)
    ids = jnp.arange(rows, dtype=jnp.int32)
    lanes = jnp.stack([ids // block, ids % block]).astype(f32)
    subs = lanes.T

    act = jax.ShapeDtypeStruct((rows, width), bf16)
    terms = jax.ShapeDtypeStruct((4, width, width), bf16)
    vm = pltpu.VMEM((rows, width), bf16)
    dist = pltpu.VMEM((rows, rows), f32)
    params = pltpu.CompilerParams(vmem_limit_bytes=VMEM_LIMIT)
    swap = functools.partial(lax.all_to_all, axis_name="pos", split_axis=0, concat_axis=0, tiled=True)

    def spread(array):
        return swap(array.reshape(ranks, block, width)).reshape(rows, width)

    up_rows = spread(cotangent.reshape(rows, width))
    q, k, v, mixed, hidden = pl.pallas_call(
        col_forward, out_shape=[act] * 5, scratch_shapes=[dist], compiler_params=params
    )(x, col_weights, cov)
    hid_rows = spread(hidden)
    spec = pl.BlockSpec(memory_space=pltpu.VMEM)
    back, row_terms = pl.pallas_call(
        row_both,
        out_shape=[act, terms],
        in_specs=[spec] * 6 + [pl.BlockSpec(memory_space=pltpu.SMEM)],
        scratch_shapes=[vm] * 9 + [dist],
        compiler_params=params,
    )(hid_rows, up_rows, row_weights, row_cov, subs, lanes, windows)
    up_cols = spread(back)
    grad, col_terms = pl.pallas_call(
        col_backward,
        out_shape=[act, terms],
        scratch_shapes=[vm] * 5 + [dist],
        compiler_params=params,
    )(x, up_cols, col_weights, cov, q, k, v, mixed)
    row_sums = reduce_rows(row_terms, ranks, me)
    col_sums = reduce_rows(col_terms, ranks, me)
    return (grad.reshape(inputs.shape), col_sums, row_sums)


def solution(mesh):
    return jax.shard_map(
        shards,
        mesh=mesh,
        in_specs=(P("grp", "pos", None), P("grp", "pos", None), P(), P(), P("grp"), P("grp"), P()),
        out_specs=(P("grp", "pos", None), P("grp", "pos", None), P("grp", "pos", None)),
        check_vma=False,
    )
```

```python
import functools

import jax
import jax.numpy as jnp
from jax import lax
from jax.experimental import pallas as pl
from jax.experimental.pallas import tpu as pltpu
from jax.sharding import PartitionSpec as P

HEADS = 8
LANES = 128
NEG = -1e30
FAR = 1e9
VMEM_LIMIT = 56 * 1024 * 1024
f32, bf16 = jnp.float32, jnp.bfloat16


def dot_nn(a, b):
    return lax.dot_general(a, b, (((1,), (0,)), ((), ())), preferred_element_type=f32)


def dot_nt(a, b):
    return lax.dot_general(a, b, (((1,), (1,)), ((), ())), preferred_element_type=f32)


def dot_tn(a, b):
    return lax.dot_general(a, b, (((0,), (0,)), ((), ())), preferred_element_type=f32)


def project(x_ref, w_ref, q_ref, k_ref, v_ref):
    x = x_ref[...]
    q_ref[...] = (dot_nn(x, w_ref[0]) * 0.125).astype(bf16)
    k_ref[...] = dot_nn(x, w_ref[1]).astype(bf16)
    v_ref[...] = dot_nn(x, w_ref[2]).astype(bf16)


def probs_t(k2, qm, dist, width):
    s = jnp.where(dist <= width, dot_nt(k2, qm), NEG)
    e = jnp.exp(s - jnp.max(s, axis=0, keepdims=True))
    return e * (1.0 / jnp.sum(e, axis=0, keepdims=True))


def halves(pair):
    lane = lax.broadcasted_iota(jnp.int32, pair.shape, 1)
    low = lane < LANES // 2
    zero = jnp.zeros_like(pair)
    return jnp.where(low, pair, zero), jnp.where(low, zero, pair)


def merge(a, b):
    lane = lax.broadcasted_iota(jnp.int32, a.shape, 1)
    return jnp.where(lane < LANES // 2, a, b)


def forward_pairs(q_ref, k_ref, v_ref, dist_ref, m_ref, p_ref):
    @pl.loop(0, HEADS // 2)
    def _(pair):
        at = pl.ds(pl.multiple_of(pair * LANES, LANES), LANES)
        k2, v2 = k_ref[:, at], v_ref[:, at]
        outs = []
        for which, qm in enumerate(halves(q_ref[:, at])):
            p = probs_t(k2, qm, dist_ref[...], 0.5)
            p_ref[pair * 2 + which] = p
            outs.append(dot_tn(p.astype(bf16), v2))
        m_ref[:, at] = merge(*outs).astype(bf16)


def backward_pairs(q_ref, k_ref, v_ref, g_ref, probs_of, m_ref, dq_ref, dk_ref, dv_ref):
    @pl.loop(0, HEADS // 2)
    def _(pair):
        at = pl.ds(pl.multiple_of(pair * LANES, LANES), LANES)
        k2, v2 = k_ref[:, at], v_ref[:, at]
        q_parts, g_parts = halves(q_ref[:, at]), halves(g_ref[:, at])
        outs, dqs, dk, dv = [], [], 0.0, 0.0
        for which in range(2):
            qm, gm = q_parts[which], g_parts[which]
            p = probs_of(pair * 2 + which, k2, qm)
            pb = p.astype(bf16)
            if m_ref is not None:
                outs.append(dot_tn(pb, v2))
            dp = dot_nt(v2, gm).astype(bf16).astype(f32)
            ds = (p * (dp - jnp.sum(dp * p, axis=0, keepdims=True))).astype(bf16)
            dv = dv + dot_nn(pb, gm)
            dk = dk + dot_nn(ds, qm)
            dqs.append(dot_tn(ds, k2))
        if m_ref is not None:
            m_ref[:, at] = merge(*outs).astype(bf16)
        dq_ref[:, at] = (merge(*dqs) * 0.125).astype(bf16)
        dk_ref[:, at] = dk.astype(bf16)
        dv_ref[:, at] = dv.astype(bf16)


def back_sum(up, w_ref, dq_ref, dk_ref, dv_ref):
    back = up.astype(f32)
    for which, grad_ref in enumerate((dq_ref, dk_ref, dv_ref)):
        back = back + dot_nt(grad_ref[...], w_ref[which])
    return back


def reverse_bits(value, bits):
    return sum(((value >> b) & 1) << (bits - 1 - b) for b in range(bits))


def kernel(
    ranks, x_ref, cot_ref, cw_ref, rw_ref, start_ref, end_ref, windows_ref,
    grad_ref, col_out, row_out,
    q_ref, k_ref, v_ref, m_ref, rq_ref, rk_ref, rv_ref, rm_ref, og_ref, g_ref,
    dq_ref, dk_ref, dv_ref, up_ref, h_ref, wide_ref, dist_ref, p_ref,
    send_buf, cot_in, hid_in, back_buf, back_in,
    col_terms, row_terms, col_got, row_got,
    swap_send, swap_recv, sum_send, sum_recv,
):
    rows = x_ref.shape[0]
    block = rows // ranks
    bits = ranks.bit_length() - 1
    part = col_terms.shape[2]
    me = lax.axis_index("pos")

    barrier = pltpu.get_barrier_semaphore()

    @pl.loop(1, ranks)
    def _(step):
        pl.semaphore_signal(barrier, inc=1, device_id={"pos": lax.rem(me + step, ranks)})

    pl.semaphore_wait(barrier, ranks - 1)

    def swap_copy(which, src, dst, peer, slot):
        return pltpu.make_async_remote_copy(
            src_ref=src.at[peer],
            dst_ref=dst.at[slot],
            send_sem=swap_send.at[which, peer],
            recv_sem=swap_recv.at[which, slot],
            device_id={"pos": peer},
        )

    def swap_start(which, src, dst):
        @pl.loop(0, ranks - 1)
        def _(step):
            shift = 1 + lax.rem(step + ranks // 2 - 1, ranks - 1)
            swap_copy(which, src, dst, lax.rem(me + shift, ranks), me).start()

        dst[me] = src[me]

    def swap_wait(which, src, dst):
        @pl.loop(1, ranks)
        def _(shift):
            peer = lax.rem(me + shift, ranks)
            swap_copy(which, src, dst, peer, peer).wait_recv()

    def swap_sent(which, src, dst):
        @pl.loop(1, ranks)
        def _(shift):
            swap_copy(which, src, dst, lax.rem(me + shift, ranks), me).wait_send()

    def scatter_blocks(value, dst):
        for r in range(ranks):
            dst[r] = value[r * block:(r + 1) * block].astype(bf16)

    def gather_blocks(src, dst):
        for r in range(ranks):
            wide_ref[r * block:(r + 1) * block, :] = src[r].astype(f32)
        dst[...] = wide_ref[...].astype(bf16)

    keeps, gives, begin = [], [], 0
    for b in range(bits):
        half = ranks >> (b + 1)
        mine = lax.rem(me // (1 << b), 2)
        gives.append(begin + (1 - mine) * half)
        begin = begin + mine * half
        keeps.append(begin)

    def sum_copy(which, terms, got, b, w):
        half = ranks >> (b + 1)
        mine = lax.rem(me // (1 << b), 2)
        return pltpu.make_async_remote_copy(
            src_ref=terms.at[w, pl.ds(gives[b], half)],
            dst_ref=got.at[w, pl.ds(ranks - 2 * half, half)],
            send_sem=sum_send.at[which, b, w],
            recv_sem=sum_recv.at[which, b, w],
            device_id={"pos": me + (1 - 2 * mine) * (1 << b)},
        )

    def put_term(terms, w, value):
        for r in range(ranks):
            terms[w, reverse_bits(r, bits)] = value[r * part:(r + 1) * part].astype(bf16)

    def sum_step(which, terms, got, out, b, w):
        half = ranks >> (b + 1)
        sum_copy(which, terms, got, b, w).wait_recv()
        held = pl.ds(keeps[b], half)
        total = terms[w, held].astype(f32) + got[w, ranks - 2 * half:ranks - half].astype(f32)
        if b == bits - 1:
            out[w] = total[0]
        else:
            terms[w, held] = total.astype(bf16)
            sum_copy(which, terms, got, b + 1, w).start()

    def row_steps(b):
        for w in (3, 0, 1, 2):
            sum_step(0, row_terms, row_got, row_out, b, w)

    swap_start(0, cot_ref, cot_in)
    at_j = lax.broadcasted_iota(jnp.int32, (rows, rows), 0)
    at_i = lax.broadcasted_iota(jnp.int32, (rows, rows), 1)
    starts, ends = start_ref[...], end_ref[...]
    covers = ((me >= starts) & (me < ends)).astype(f32)
    cov = jnp.sum(jnp.where(at_j == at_i, covers, 0.0), axis=1, keepdims=True)
    dist_ref[...] = jnp.where((cov > 0.5) | (at_i == at_j), 0.0, FAR)
    project(x_ref, cw_ref, q_ref, k_ref, v_ref)
    forward_pairs(q_ref, k_ref, v_ref, dist_ref, m_ref, p_ref)
    wide_ref[...] = x_ref[...].astype(f32) + dot_nn(m_ref[...], cw_ref[3]) * cov
    scatter_blocks(wide_ref[...], send_buf)
    swap_start(1, send_buf, hid_in)

    sub = lax.broadcasted_iota(jnp.int32, (rows, 1), 0).astype(f32)
    lane = lax.broadcasted_iota(jnp.int32, (1, rows), 1).astype(f32)
    place_j, place_i = jnp.floor((sub + 0.5) / block), jnp.floor((lane + 0.5) / block)
    read_j, read_i = sub - block * place_j, lane - block * place_i
    own = lane == me.astype(f32) * block + read_j
    start_j = jnp.sum(jnp.where(own, starts.astype(f32), 0.0), axis=1, keepdims=True)
    end_j = jnp.sum(jnp.where(own, ends.astype(f32), 0.0), axis=1, keepdims=True)
    row_cov = ((place_j >= start_j) & (place_j < end_j)).astype(f32)
    gap = jnp.abs(place_j - place_i)
    dist_ref[...] = jnp.where((read_j == read_i) & ((row_cov > 0.5) | (gap == 0.0)), gap, FAR)
    swap_wait(0, cot_ref, cot_in)
    gather_blocks(cot_in, up_ref)
    og_ref[...] = (up_ref[...].astype(f32) * row_cov).astype(bf16)
    g_ref[...] = dot_nt(og_ref[...], rw_ref[3]).astype(bf16)
    swap_wait(1, send_buf, hid_in)
    gather_blocks(hid_in, h_ref)
    project(h_ref, rw_ref, rq_ref, rk_ref, rv_ref)
    backward_pairs(
        rq_ref, rk_ref, rv_ref, g_ref,
        lambda head, k2, qm: probs_t(k2, qm, dist_ref[...], windows_ref[head].astype(f32)),
        rm_ref, dq_ref, dk_ref, dv_ref,
    )
    wide_ref[...] = back_sum(up_ref[...], rw_ref, dq_ref, dk_ref, dv_ref)
    scatter_blocks(wide_ref[...], back_buf)
    swap_start(2, back_buf, back_in)
    for w, left, right in (
        (3, rm_ref, og_ref), (0, h_ref, dq_ref), (1, h_ref, dk_ref), (2, h_ref, dv_ref)
    ):
        put_term(row_terms, w, dot_tn(left[...], right[...]))
        sum_copy(0, row_terms, row_got, 0, w).start()
    row_steps(0)

    swap_wait(2, back_buf, back_in)
    gather_blocks(back_in, up_ref)
    og_ref[...] = (up_ref[...].astype(f32) * cov).astype(bf16)
    put_term(col_terms, 3, dot_tn(m_ref[...], og_ref[...]))
    sum_copy(1, col_terms, col_got, 0, 3).start()
    g_ref[...] = dot_nt(og_ref[...], cw_ref[3]).astype(bf16)
    row_steps(1)
    backward_pairs(
        q_ref, k_ref, v_ref, g_ref, lambda head, k2, qm: p_ref[head], None, dq_ref, dk_ref, dv_ref
    )
    sum_step(1, col_terms, col_got, col_out, 0, 3)
    for w, right in enumerate((dq_ref, dk_ref, dv_ref)):
        put_term(col_terms, w, dot_tn(x_ref[...], right[...]))
        sum_copy(1, col_terms, col_got, 0, w).start()
        if w > 0:
            sum_step(1, col_terms, col_got, col_out, 0, w - 1)
    sum_step(1, col_terms, col_got, col_out, 0, 2)
    for b in range(2, bits):
        row_steps(b)
    grad_ref[...] = back_sum(up_ref[...], cw_ref, dq_ref, dk_ref, dv_ref).astype(bf16)
    for b in range(1, bits):
        for w in (3, 0, 1, 2):
            sum_step(1, col_terms, col_got, col_out, b, w)

    swap_sent(0, cot_ref, cot_in)
    swap_sent(1, send_buf, hid_in)
    swap_sent(2, back_buf, back_in)
    for b in range(bits):
        for w in range(4):
            sum_copy(0, row_terms, row_got, b, w).wait_send()
            sum_copy(1, col_terms, col_got, b, w).wait_send()


def shards(inputs, cotangent, col_weights, row_weights, read_start, read_end, windows):
    rows, local_pos, width = inputs.shape
    ranks = lax.axis_size("pos")
    block, part, bits = rows // ranks, width // ranks, ranks.bit_length() - 1
    act = pltpu.VMEM((rows, width), bf16)
    blocks = pltpu.VMEM((ranks, block, width), bf16)
    terms = pltpu.VMEM((4, ranks, part, width), bf16)
    sums = jax.ShapeDtypeStruct((4, part, width), f32)
    spec = pl.BlockSpec(memory_space=pltpu.VMEM)
    grad, col_sums, row_sums = pl.pallas_call(
        functools.partial(kernel, ranks),
        out_shape=[jax.ShapeDtypeStruct((rows, width), bf16), sums, sums],
        in_specs=[spec] * 6 + [pl.BlockSpec(memory_space=pltpu.SMEM)],
        out_specs=[spec] * 3,
        scratch_shapes=[act] * 15
        + [pltpu.VMEM((rows, width), f32), pltpu.VMEM((rows, rows), f32)]
        + [pltpu.VMEM((HEADS, rows, rows), f32)]
        + [blocks] * 5
        + [terms] * 4
        + [pltpu.SemaphoreType.DMA((3, ranks))] * 2
        + [pltpu.SemaphoreType.DMA((2, bits, 4))] * 2,
        compiler_params=pltpu.CompilerParams(
            vmem_limit_bytes=VMEM_LIMIT, collective_id=0, has_side_effects=True
        ),
    )(
        inputs.reshape(rows, width),
        cotangent.reshape(ranks, block, width),
        col_weights,
        row_weights,
        read_start.reshape(1, rows),
        read_end.reshape(1, rows),
        windows,
    )
    return (grad.reshape(inputs.shape), col_sums, row_sums)


def solution(mesh):
    return jax.shard_map(
        shards,
        mesh=mesh,
        in_specs=(P("grp", "pos", None), P("grp", "pos", None), P(), P(), P("grp"), P("grp"), P()),
        out_specs=(P("grp", "pos", None), P("grp", "pos", None), P("grp", "pos", None)),
        check_vma=False,
    )
```

```python
import functools

import jax
import jax.numpy as jnp
from jax import lax
from jax.experimental import pallas as pl
from jax.experimental.pallas import tpu as pltpu
from jax.sharding import PartitionSpec as P

HEADS = 8
LANES = 128
NEG = -1e30
FAR = 1e9
LATE_NEAR = (0,)
VMEM_LIMIT = 56 * 1024 * 1024
f32, bf16 = jnp.float32, jnp.bfloat16


def dot_nn(a, b):
    return lax.dot_general(a, b, (((1,), (0,)), ((), ())), preferred_element_type=f32)


def dot_nt(a, b):
    return lax.dot_general(a, b, (((1,), (1,)), ((), ())), preferred_element_type=f32)


def dot_tn(a, b):
    return lax.dot_general(a, b, (((0,), (0,)), ((), ())), preferred_element_type=f32)


def project(x_ref, w_ref, q_ref, k_ref, v_ref):
    x = x_ref[...]
    q_ref[...] = (dot_nn(x, w_ref[0]) * 0.125).astype(bf16)
    k_ref[...] = dot_nn(x, w_ref[1]).astype(bf16)
    v_ref[...] = dot_nn(x, w_ref[2]).astype(bf16)


def probs_t(k2, qm, dist, width):
    s = jnp.where(dist <= width, dot_nt(k2, qm), NEG)
    e = jnp.exp(s - jnp.max(s, axis=0, keepdims=True))
    return e * (1.0 / jnp.sum(e, axis=0, keepdims=True))


def halves(pair):
    lane = lax.broadcasted_iota(jnp.int32, pair.shape, 1)
    low = lane < LANES // 2
    zero = jnp.zeros_like(pair)
    return jnp.where(low, pair, zero), jnp.where(low, zero, pair)


def merge(a, b):
    lane = lax.broadcasted_iota(jnp.int32, a.shape, 1)
    return jnp.where(lane < LANES // 2, a, b)


def forward_pairs(q_ref, k_ref, v_ref, dist_ref, m_ref, p_ref):
    @pl.loop(0, HEADS // 2)
    def _(pair):
        at = pl.ds(pl.multiple_of(pair * LANES, LANES), LANES)
        k2, v2 = k_ref[:, at], v_ref[:, at]
        outs = []
        for which, qm in enumerate(halves(q_ref[:, at])):
            p = probs_t(k2, qm, dist_ref[...], 0.5)
            p_ref[pair * 2 + which] = p
            outs.append(dot_tn(p.astype(bf16), v2))
        m_ref[:, at] = merge(*outs).astype(bf16)


def backward_pairs(q_ref, k_ref, v_ref, g_ref, probs_of, m_ref, dq_ref, dk_ref, dv_ref):
    @pl.loop(0, HEADS // 2)
    def _(pair):
        at = pl.ds(pl.multiple_of(pair * LANES, LANES), LANES)
        k2, v2 = k_ref[:, at], v_ref[:, at]
        q_parts, g_parts = halves(q_ref[:, at]), halves(g_ref[:, at])
        outs, dqs, dk, dv = [], [], 0.0, 0.0
        for which in range(2):
            qm, gm = q_parts[which], g_parts[which]
            p = probs_of(pair * 2 + which, k2, qm)
            pb = p.astype(bf16)
            if m_ref is not None:
                outs.append(dot_tn(pb, v2))
            dp = dot_nt(v2, gm).astype(bf16).astype(f32)
            ds = (p * (dp - jnp.sum(dp * p, axis=0, keepdims=True))).astype(bf16)
            dv = dv + dot_nn(pb, gm)
            dk = dk + dot_nn(ds, qm)
            dqs.append(dot_tn(ds, k2))
        if m_ref is not None:
            m_ref[:, at] = merge(*outs).astype(bf16)
        dq_ref[:, at] = (merge(*dqs) * 0.125).astype(bf16)
        dk_ref[:, at] = dk.astype(bf16)
        dv_ref[:, at] = dv.astype(bf16)


def back_sum(up, w_ref, dq_ref, dk_ref, dv_ref):
    back = up.astype(f32)
    for which, grad_ref in enumerate((dq_ref, dk_ref, dv_ref)):
        back = back + dot_nt(grad_ref[...], w_ref[which])
    return back


def kernel(
    ranks, x_ref, cot_ref, cw_ref, rw_ref, start_ref, end_ref, windows_ref,
    grad_ref, col_out, row_out,
    q_ref, k_ref, v_ref, m_ref, rq_ref, rk_ref, rv_ref, rm_ref, og_ref, g_ref,
    dq_ref, dk_ref, dv_ref, up_ref, h_ref, wide_ref, dist_ref, p_ref,
    send_buf, cot_in, hid_in, back_buf, back_in,
    col_terms, row_terms, col_got, row_got,
    swap_send, swap_recv, sum_send, sum_recv,
):
    rows = x_ref.shape[0]
    block = rows // ranks
    bits = ranks.bit_length() - 1
    part = col_terms.shape[2]
    me = lax.axis_index("pos")

    barrier = pltpu.get_barrier_semaphore()

    @pl.loop(1, ranks)
    def _(step):
        pl.semaphore_signal(barrier, inc=1, device_id={"pos": lax.rem(me + step, ranks)})

    pl.semaphore_wait(barrier, ranks - 1)

    def swap_copy(which, src, dst, peer, slot):
        return pltpu.make_async_remote_copy(
            src_ref=src.at[peer],
            dst_ref=dst.at[slot],
            send_sem=swap_send.at[which, peer],
            recv_sem=swap_recv.at[which, slot],
            device_id={"pos": peer},
        )

    def swap_start(which, src, dst):
        @pl.loop(0, ranks - 1)
        def _(step):
            shift = 1 + lax.rem(step + ranks // 2 - 1, ranks - 1)
            swap_copy(which, src, dst, lax.rem(me + shift, ranks), me).start()

        dst[me] = src[me]

    def swap_wait(which, src, dst):
        @pl.loop(1, ranks)
        def _(shift):
            peer = lax.rem(me + shift, ranks)
            swap_copy(which, src, dst, peer, peer).wait_recv()

    def swap_sent(which, src, dst):
        @pl.loop(1, ranks)
        def _(shift):
            swap_copy(which, src, dst, lax.rem(me + shift, ranks), me).wait_send()

    def scatter_blocks(value, dst):
        for r in range(ranks):
            dst[r] = value[r * block:(r + 1) * block].astype(bf16)

    def gather_blocks(src, dst):
        for r in range(ranks):
            wide_ref[r * block:(r + 1) * block, :] = src[r].astype(f32)
        dst[...] = wide_ref[...].astype(bf16)

    orders = [list(range(bits)) for _ in range(4)]
    for w in LATE_NEAR:
        orders[w] = [0] + list(range(2, bits)) + [1]
    keeps, gives, partners = [], [], []
    for w in range(4):
        begin, keep, give, partner = 0, [], [], []
        for b, bit in enumerate(orders[w]):
            half = ranks >> (b + 1)
            mine = lax.rem(me // (1 << bit), 2)
            give.append(begin + (1 - mine) * half)
            begin = begin + mine * half
            keep.append(begin)
            partner.append(me + (1 - 2 * mine) * (1 << bit))
        keeps.append(keep)
        gives.append(give)
        partners.append(partner)

    def sum_copy(which, terms, got, b, w):
        half = ranks >> (b + 1)
        return pltpu.make_async_remote_copy(
            src_ref=terms.at[w, pl.ds(gives[w][b], half)],
            dst_ref=got.at[w, pl.ds(ranks - 2 * half, half)],
            send_sem=sum_send.at[which, b, w],
            recv_sem=sum_recv.at[which, b, w],
            device_id={"pos": partners[w][b]},
        )

    def put_term(terms, w, value):
        for r in range(ranks):
            slot = sum(((r >> bit) & 1) << (bits - 1 - b) for b, bit in enumerate(orders[w]))
            terms[w, slot] = value[r * part:(r + 1) * part].astype(bf16)

    def sum_step(which, terms, got, out, b, w):
        half = ranks >> (b + 1)
        sum_copy(which, terms, got, b, w).wait_recv()
        held = pl.ds(keeps[w][b], half)
        total = terms[w, held].astype(f32) + got[w, ranks - 2 * half:ranks - half].astype(f32)
        if b == bits - 1:
            out[w] = total[0]
        else:
            terms[w, held] = total.astype(bf16)
            sum_copy(which, terms, got, b + 1, w).start()

    def row_steps(b):
        for w in (3, 0, 1, 2):
            sum_step(0, row_terms, row_got, row_out, b, w)

    swap_start(0, cot_ref, cot_in)
    at_j = lax.broadcasted_iota(jnp.int32, (rows, rows), 0)
    at_i = lax.broadcasted_iota(jnp.int32, (rows, rows), 1)
    starts, ends = start_ref[...], end_ref[...]
    covers = ((me >= starts) & (me < ends)).astype(f32)
    cov = jnp.sum(jnp.where(at_j == at_i, covers, 0.0), axis=1, keepdims=True)
    dist_ref[...] = jnp.where((cov > 0.5) | (at_i == at_j), 0.0, FAR)
    project(x_ref, cw_ref, q_ref, k_ref, v_ref)
    forward_pairs(q_ref, k_ref, v_ref, dist_ref, m_ref, p_ref)
    wide_ref[...] = x_ref[...].astype(f32) + dot_nn(m_ref[...], cw_ref[3]) * cov
    scatter_blocks(wide_ref[...], send_buf)
    swap_start(1, send_buf, hid_in)

    sub = lax.broadcasted_iota(jnp.int32, (rows, 1), 0).astype(f32)
    lane = lax.broadcasted_iota(jnp.int32, (1, rows), 1).astype(f32)
    place_j, place_i = jnp.floor((sub + 0.5) / block), jnp.floor((lane + 0.5) / block)
    read_j, read_i = sub - block * place_j, lane - block * place_i
    own = lane == me.astype(f32) * block + read_j
    start_j = jnp.sum(jnp.where(own, starts.astype(f32), 0.0), axis=1, keepdims=True)
    end_j = jnp.sum(jnp.where(own, ends.astype(f32), 0.0), axis=1, keepdims=True)
    row_cov = ((place_j >= start_j) & (place_j < end_j)).astype(f32)
    gap = jnp.abs(place_j - place_i)
    dist_ref[...] = jnp.where((read_j == read_i) & ((row_cov > 0.5) | (gap == 0.0)), gap, FAR)
    swap_wait(0, cot_ref, cot_in)
    gather_blocks(cot_in, up_ref)
    og_ref[...] = (up_ref[...].astype(f32) * row_cov).astype(bf16)
    g_ref[...] = dot_nt(og_ref[...], rw_ref[3]).astype(bf16)
    swap_wait(1, send_buf, hid_in)
    gather_blocks(hid_in, h_ref)
    project(h_ref, rw_ref, rq_ref, rk_ref, rv_ref)
    backward_pairs(
        rq_ref, rk_ref, rv_ref, g_ref,
        lambda head, k2, qm: probs_t(k2, qm, dist_ref[...], windows_ref[head].astype(f32)),
        rm_ref, dq_ref, dk_ref, dv_ref,
    )
    wide_ref[...] = back_sum(up_ref[...], rw_ref, dq_ref, dk_ref, dv_ref)
    scatter_blocks(wide_ref[...], back_buf)
    swap_start(2, back_buf, back_in)
    for w, left, right in (
        (3, rm_ref, og_ref), (0, h_ref, dq_ref), (1, h_ref, dk_ref), (2, h_ref, dv_ref)
    ):
        put_term(row_terms, w, dot_tn(left[...], right[...]))
        sum_copy(0, row_terms, row_got, 0, w).start()

    swap_wait(2, back_buf, back_in)
    gather_blocks(back_in, up_ref)
    row_steps(0)
    og_ref[...] = (up_ref[...].astype(f32) * cov).astype(bf16)
    put_term(col_terms, 3, dot_tn(m_ref[...], og_ref[...]))
    sum_copy(1, col_terms, col_got, 0, 3).start()
    g_ref[...] = dot_nt(og_ref[...], cw_ref[3]).astype(bf16)
    backward_pairs(
        q_ref, k_ref, v_ref, g_ref, lambda head, k2, qm: p_ref[head], None, dq_ref, dk_ref, dv_ref
    )
    row_steps(1)
    sum_step(1, col_terms, col_got, col_out, 0, 3)
    for w, right in enumerate((dq_ref, dk_ref, dv_ref)):
        put_term(col_terms, w, dot_tn(x_ref[...], right[...]))
        sum_copy(1, col_terms, col_got, 0, w).start()
        if w > 0:
            sum_step(1, col_terms, col_got, col_out, 0, w - 1)
    sum_step(1, col_terms, col_got, col_out, 0, 2)
    for b in range(2, bits):
        row_steps(b)
    grad_ref[...] = back_sum(up_ref[...], cw_ref, dq_ref, dk_ref, dv_ref).astype(bf16)
    for b in range(1, bits):
        for w in (3, 0, 1, 2):
            sum_step(1, col_terms, col_got, col_out, b, w)

    swap_sent(0, cot_ref, cot_in)
    swap_sent(1, send_buf, hid_in)
    swap_sent(2, back_buf, back_in)
    for b in range(bits):
        for w in range(4):
            sum_copy(0, row_terms, row_got, b, w).wait_send()
            sum_copy(1, col_terms, col_got, b, w).wait_send()


def shards(inputs, cotangent, col_weights, row_weights, read_start, read_end, windows):
    rows, local_pos, width = inputs.shape
    ranks = lax.axis_size("pos")
    block, part, bits = rows // ranks, width // ranks, ranks.bit_length() - 1
    act = pltpu.VMEM((rows, width), bf16)
    blocks = pltpu.VMEM((ranks, block, width), bf16)
    terms = pltpu.VMEM((4, ranks, part, width), bf16)
    sums = jax.ShapeDtypeStruct((4, part, width), f32)
    spec = pl.BlockSpec(memory_space=pltpu.VMEM)
    grad, col_sums, row_sums = pl.pallas_call(
        functools.partial(kernel, ranks),
        out_shape=[jax.ShapeDtypeStruct((rows, width), bf16), sums, sums],
        in_specs=[spec] * 6 + [pl.BlockSpec(memory_space=pltpu.SMEM)],
        out_specs=[spec] * 3,
        scratch_shapes=[act] * 15
        + [pltpu.VMEM((rows, width), f32), pltpu.VMEM((rows, rows), f32)]
        + [pltpu.VMEM((HEADS, rows, rows), f32)]
        + [blocks] * 5
        + [terms] * 4
        + [pltpu.SemaphoreType.DMA((3, ranks))] * 2
        + [pltpu.SemaphoreType.DMA((2, bits, 4))] * 2,
        compiler_params=pltpu.CompilerParams(
            vmem_limit_bytes=VMEM_LIMIT, collective_id=0, has_side_effects=True
        ),
    )(
        inputs.reshape(rows, width),
        cotangent.reshape(ranks, block, width),
        col_weights,
        row_weights,
        read_start.reshape(1, rows),
        read_end.reshape(1, rows),
        windows,
    )
    return (grad.reshape(inputs.shape), col_sums, row_sums)


def solution(mesh):
    return jax.shard_map(
        shards,
        mesh=mesh,
        in_specs=(P("grp", "pos", None), P("grp", "pos", None), P(), P(), P("grp"), P("grp"), P()),
        out_specs=(P("grp", "pos", None), P("grp", "pos", None), P("grp", "pos", None)),
        check_vma=False,
    )
```

```python
import functools

import jax
import jax.numpy as jnp
from jax import lax
from jax.experimental import pallas as pl
from jax.experimental.pallas import tpu as pltpu
from jax.sharding import PartitionSpec as P

HEADS = 8
LANES = 128
NEG = -1e30
FAR = 1e9
LATE_NEAR = (0,)
VMEM_LIMIT = 56 * 1024 * 1024
f32, bf16 = jnp.float32, jnp.bfloat16


def dot_nn(a, b):
    return lax.dot_general(a, b, (((1,), (0,)), ((), ())), preferred_element_type=f32)


def dot_nt(a, b):
    return lax.dot_general(a, b, (((1,), (1,)), ((), ())), preferred_element_type=f32)


def dot_tn(a, b):
    return lax.dot_general(a, b, (((0,), (0,)), ((), ())), preferred_element_type=f32)


def project(x_ref, w_ref, q_ref, k_ref, v_ref):
    x = x_ref[...]
    q_ref[...] = (dot_nn(x, w_ref[0]) * 0.125).astype(bf16)
    k_ref[...] = dot_nn(x, w_ref[1]).astype(bf16)
    v_ref[...] = dot_nn(x, w_ref[2]).astype(bf16)


def probs_t(k2, qm, dist, width):
    s = jnp.where(dist <= width, dot_nt(k2, qm), NEG)
    e = jnp.exp(s - jnp.max(s, axis=0, keepdims=True))
    return e * (1.0 / jnp.sum(e, axis=0, keepdims=True))


def halves(pair):
    lane = lax.broadcasted_iota(jnp.int32, pair.shape, 1)
    low = lane < LANES // 2
    zero = jnp.zeros_like(pair)
    return jnp.where(low, pair, zero), jnp.where(low, zero, pair)


def merge(a, b):
    lane = lax.broadcasted_iota(jnp.int32, a.shape, 1)
    return jnp.where(lane < LANES // 2, a, b)


def forward_pairs(q_ref, k_ref, v_ref, dist_ref, m_ref, p_ref):
    @pl.loop(0, HEADS // 2)
    def _(pair):
        at = pl.ds(pl.multiple_of(pair * LANES, LANES), LANES)
        k2, v2 = k_ref[:, at], v_ref[:, at]
        outs = []
        for which, qm in enumerate(halves(q_ref[:, at])):
            p = probs_t(k2, qm, dist_ref[...], 0.5)
            p_ref[pair * 2 + which] = p
            outs.append(dot_tn(p.astype(bf16), v2))
        m_ref[:, at] = merge(*outs).astype(bf16)


def backward_pairs(q_ref, k_ref, v_ref, g_ref, probs_of, m_ref, dq_ref, dk_ref, dv_ref):
    @pl.loop(0, HEADS // 2)
    def _(pair):
        at = pl.ds(pl.multiple_of(pair * LANES, LANES), LANES)
        k2, v2 = k_ref[:, at], v_ref[:, at]
        q_parts, g_parts = halves(q_ref[:, at]), halves(g_ref[:, at])
        outs, dqs, dk, dv = [], [], 0.0, 0.0
        for which in range(2):
            qm, gm = q_parts[which], g_parts[which]
            p = probs_of(pair * 2 + which, k2, qm)
            pb = p.astype(bf16)
            if m_ref is not None:
                outs.append(dot_tn(pb, v2))
            dp = dot_nt(v2, gm).astype(bf16).astype(f32)
            ds = (p * (dp - jnp.sum(dp * p, axis=0, keepdims=True))).astype(bf16)
            dv = dv + dot_nn(pb, gm)
            dk = dk + dot_nn(ds, qm)
            dqs.append(dot_tn(ds, k2))
        if m_ref is not None:
            m_ref[:, at] = merge(*outs).astype(bf16)
        dq_ref[:, at] = (merge(*dqs) * 0.125).astype(bf16)
        dk_ref[:, at] = dk.astype(bf16)
        dv_ref[:, at] = dv.astype(bf16)


def back_sum(up, w_ref, dq_ref, dk_ref, dv_ref):
    back = up.astype(f32)
    for which, grad_ref in enumerate((dq_ref, dk_ref, dv_ref)):
        back = back + dot_nt(grad_ref[...], w_ref[which])
    return back


def kernel(
    ranks, x_ref, cot_ref, cw_ref, rw_ref, start_ref, end_ref, windows_ref,
    grad_ref, col_out, row_out,
    q_ref, k_ref, v_ref, m_ref, rq_ref, rk_ref, rv_ref, rm_ref, og_ref, g_ref,
    dq_ref, dk_ref, dv_ref, up_ref, h_ref, wide_ref, dist_ref, p_ref,
    send_buf, cot_in, hid_in, back_buf, back_in,
    col_terms, row_terms, col_got, row_got,
    swap_send, swap_recv, sum_send, sum_recv,
):
    rows = x_ref.shape[0]
    block = rows // ranks
    bits = ranks.bit_length() - 1
    part = col_terms.shape[2]
    me = lax.axis_index("pos")

    barrier = pltpu.get_barrier_semaphore()

    @pl.loop(1, ranks)
    def _(step):
        pl.semaphore_signal(barrier, inc=1, device_id={"pos": lax.rem(me + step, ranks)})

    pl.semaphore_wait(barrier, ranks - 1)

    def swap_copy(which, src, dst, peer, slot):
        return pltpu.make_async_remote_copy(
            src_ref=src.at[peer],
            dst_ref=dst.at[slot],
            send_sem=swap_send.at[which, peer],
            recv_sem=swap_recv.at[which, slot],
            device_id={"pos": peer},
        )

    def swap_start(which, src, dst):
        @pl.loop(0, ranks - 1)
        def _(step):
            shift = step + 1
            swap_copy(which, src, dst, lax.rem(me + shift, ranks), me).start()

        dst[me] = src[me]

    def swap_wait(which, src, dst):
        @pl.loop(1, ranks)
        def _(shift):
            peer = lax.rem(me + shift, ranks)
            swap_copy(which, src, dst, peer, peer).wait_recv()

    def swap_sent(which, src, dst):
        @pl.loop(1, ranks)
        def _(shift):
            swap_copy(which, src, dst, lax.rem(me + shift, ranks), me).wait_send()

    def scatter_blocks(value, dst):
        for r in range(ranks):
            dst[r] = value[r * block:(r + 1) * block].astype(bf16)

    def gather_blocks(src, dst):
        for r in range(ranks):
            wide_ref[r * block:(r + 1) * block, :] = src[r].astype(f32)
        dst[...] = wide_ref[...].astype(bf16)

    orders = [list(range(bits)) for _ in range(4)]
    for w in LATE_NEAR:
        orders[w] = [0] + list(range(2, bits)) + [1]
    keeps, gives, partners = [], [], []
    for w in range(4):
        begin, keep, give, partner = 0, [], [], []
        for b, bit in enumerate(orders[w]):
            half = ranks >> (b + 1)
            mine = lax.rem(me // (1 << bit), 2)
            give.append(begin + (1 - mine) * half)
            begin = begin + mine * half
            keep.append(begin)
            partner.append(me + (1 - 2 * mine) * (1 << bit))
        keeps.append(keep)
        gives.append(give)
        partners.append(partner)

    def sum_copy(which, terms, got, b, w):
        half = ranks >> (b + 1)
        return pltpu.make_async_remote_copy(
            src_ref=terms.at[w, pl.ds(gives[w][b], half)],
            dst_ref=got.at[w, pl.ds(ranks - 2 * half, half)],
            send_sem=sum_send.at[which, b, w],
            recv_sem=sum_recv.at[which, b, w],
            device_id={"pos": partners[w][b]},
        )

    def put_term(terms, w, value):
        for r in range(ranks):
            slot = sum(((r >> bit) & 1) << (bits - 1 - b) for b, bit in enumerate(orders[w]))
            terms[w, slot] = value[r * part:(r + 1) * part].astype(bf16)

    def sum_step(which, terms, got, out, b, w):
        half = ranks >> (b + 1)
        sum_copy(which, terms, got, b, w).wait_recv()
        held = pl.ds(keeps[w][b], half)
        total = terms[w, held].astype(f32) + got[w, ranks - 2 * half:ranks - half].astype(f32)
        if b == bits - 1:
            out[w] = total[0]
        else:
            terms[w, held] = total.astype(bf16)
            sum_copy(which, terms, got, b + 1, w).start()

    def row_steps(b):
        for w in (3, 0, 1, 2):
            sum_step(0, row_terms, row_got, row_out, b, w)

    swap_start(0, cot_ref, cot_in)
    at_j = lax.broadcasted_iota(jnp.int32, (rows, rows), 0)
    at_i = lax.broadcasted_iota(jnp.int32, (rows, rows), 1)
    starts, ends = start_ref[...], end_ref[...]
    covers = ((me >= starts) & (me < ends)).astype(f32)
    cov = jnp.sum(jnp.where(at_j == at_i, covers, 0.0), axis=1, keepdims=True)
    dist_ref[...] = jnp.where((cov > 0.5) | (at_i == at_j), 0.0, FAR)
    project(x_ref, cw_ref, q_ref, k_ref, v_ref)
    forward_pairs(q_ref, k_ref, v_ref, dist_ref, m_ref, p_ref)
    wide_ref[...] = x_ref[...].astype(f32) + dot_nn(m_ref[...], cw_ref[3]) * cov
    scatter_blocks(wide_ref[...], send_buf)
    swap_start(1, send_buf, hid_in)

    sub = lax.broadcasted_iota(jnp.int32, (rows, 1), 0).astype(f32)
    lane = lax.broadcasted_iota(jnp.int32, (1, rows), 1).astype(f32)
    place_j, place_i = jnp.floor((sub + 0.5) / block), jnp.floor((lane + 0.5) / block)
    read_j, read_i = sub - block * place_j, lane - block * place_i
    own = lane == me.astype(f32) * block + read_j
    start_j = jnp.sum(jnp.where(own, starts.astype(f32), 0.0), axis=1, keepdims=True)
    end_j = jnp.sum(jnp.where(own, ends.astype(f32), 0.0), axis=1, keepdims=True)
    row_cov = ((place_j >= start_j) & (place_j < end_j)).astype(f32)
    gap = jnp.abs(place_j - place_i)
    dist_ref[...] = jnp.where((read_j == read_i) & ((row_cov > 0.5) | (gap == 0.0)), gap, FAR)
    swap_wait(0, cot_ref, cot_in)
    gather_blocks(cot_in, up_ref)
    og_ref[...] = (up_ref[...].astype(f32) * row_cov).astype(bf16)
    g_ref[...] = dot_nt(og_ref[...], rw_ref[3]).astype(bf16)
    swap_wait(1, send_buf, hid_in)
    gather_blocks(hid_in, h_ref)
    project(h_ref, rw_ref, rq_ref, rk_ref, rv_ref)
    backward_pairs(
        rq_ref, rk_ref, rv_ref, g_ref,
        lambda head, k2, qm: probs_t(k2, qm, dist_ref[...], windows_ref[head].astype(f32)),
        rm_ref, dq_ref, dk_ref, dv_ref,
    )
    wide_ref[...] = back_sum(up_ref[...], rw_ref, dq_ref, dk_ref, dv_ref)
    scatter_blocks(wide_ref[...], back_buf)
    swap_start(2, back_buf, back_in)
    for w, left, right in (
        (3, rm_ref, og_ref), (0, h_ref, dq_ref), (1, h_ref, dk_ref), (2, h_ref, dv_ref)
    ):
        put_term(row_terms, w, dot_tn(left[...], right[...]))
        sum_copy(0, row_terms, row_got, 0, w).start()

    swap_wait(2, back_buf, back_in)
    gather_blocks(back_in, up_ref)
    row_steps(0)
    og_ref[...] = (up_ref[...].astype(f32) * cov).astype(bf16)
    put_term(col_terms, 3, dot_tn(m_ref[...], og_ref[...]))
    sum_copy(1, col_terms, col_got, 0, 3).start()
    g_ref[...] = dot_nt(og_ref[...], cw_ref[3]).astype(bf16)
    backward_pairs(
        q_ref, k_ref, v_ref, g_ref, lambda head, k2, qm: p_ref[head], None, dq_ref, dk_ref, dv_ref
    )
    row_steps(1)
    sum_step(1, col_terms, col_got, col_out, 0, 3)
    for w, right in enumerate((dq_ref, dk_ref, dv_ref)):
        put_term(col_terms, w, dot_tn(x_ref[...], right[...]))
        sum_copy(1, col_terms, col_got, 0, w).start()
        if w > 0:
            sum_step(1, col_terms, col_got, col_out, 0, w - 1)
    sum_step(1, col_terms, col_got, col_out, 0, 2)
    for b in range(2, bits):
        row_steps(b)
    grad_ref[...] = back_sum(up_ref[...], cw_ref, dq_ref, dk_ref, dv_ref).astype(bf16)
    for b in range(1, bits):
        for w in (3, 0, 1, 2):
            sum_step(1, col_terms, col_got, col_out, b, w)

    swap_sent(0, cot_ref, cot_in)
    swap_sent(1, send_buf, hid_in)
    swap_sent(2, back_buf, back_in)
    for b in range(bits):
        for w in range(4):
            sum_copy(0, row_terms, row_got, b, w).wait_send()
            sum_copy(1, col_terms, col_got, b, w).wait_send()


def shards(inputs, cotangent, col_weights, row_weights, read_start, read_end, windows):
    rows, local_pos, width = inputs.shape
    ranks = lax.axis_size("pos")
    block, part, bits = rows // ranks, width // ranks, ranks.bit_length() - 1
    act = pltpu.VMEM((rows, width), bf16)
    blocks = pltpu.VMEM((ranks, block, width), bf16)
    terms = pltpu.VMEM((4, ranks, part, width), bf16)
    sums = jax.ShapeDtypeStruct((4, part, width), f32)
    spec = pl.BlockSpec(memory_space=pltpu.VMEM)
    grad, col_sums, row_sums = pl.pallas_call(
        functools.partial(kernel, ranks),
        out_shape=[jax.ShapeDtypeStruct((rows, width), bf16), sums, sums],
        in_specs=[spec] * 6 + [pl.BlockSpec(memory_space=pltpu.SMEM)],
        out_specs=[spec] * 3,
        scratch_shapes=[act] * 15
        + [pltpu.VMEM((rows, width), f32), pltpu.VMEM((rows, rows), f32)]
        + [pltpu.VMEM((HEADS, rows, rows), f32)]
        + [blocks] * 5
        + [terms] * 4
        + [pltpu.SemaphoreType.DMA((3, ranks))] * 2
        + [pltpu.SemaphoreType.DMA((2, bits, 4))] * 2,
        compiler_params=pltpu.CompilerParams(
            vmem_limit_bytes=VMEM_LIMIT, collective_id=0, has_side_effects=True
        ),
    )(
        inputs.reshape(rows, width),
        cotangent.reshape(ranks, block, width),
        col_weights,
        row_weights,
        read_start.reshape(1, rows),
        read_end.reshape(1, rows),
        windows,
    )
    return (grad.reshape(inputs.shape), col_sums, row_sums)


def solution(mesh):
    return jax.shard_map(
        shards,
        mesh=mesh,
        in_specs=(P("grp", "pos", None), P("grp", "pos", None), P(), P(), P("grp"), P("grp"), P()),
        out_specs=(P("grp", "pos", None), P("grp", "pos", None), P("grp", "pos", None)),
        check_vma=False,
    )
```
